32 devices in a mesh: cell: 8 (over y, x, core), band: 4 (over z).
Axes of the slice: x: 2, y: 2, z: 4, core: 2. Of those that a mesh axis runs over, the one named last changes fastest.
Arguments:
- waves: float32 [192, 9464], P('band', 'cell'), may hold values from -6 to 6
- cell_matrix: float32 [32, 343, 343], P('cell')
- node_map: int32 [32, 343], P('cell'), may hold values from 0 to 1182, as said below
- share_list: int32 [8, 2, 169], P('cell'), may hold values from 0 to 1182, as said below
- contacts: int32 [2, 128], P(None, 'cell'), may hold values from 0 to 31, as said below
- proj_values: float32 [128, 8, 343], P('cell'), may hold values from -0.3125 to 0.3125
- coupling: float32 [32, 8], replicated, may hold values from -1 to 1
- proj_count: int32 [32], replicated, may hold values from 1 to 8
- mass: float32 [9464], P('cell'), may hold values from 0.5 to 2
Outputs:
- filtered: float32 [192, 9464], P('band', 'cell')
- gram: float32 [192, 192], P('band')
The draws below stay inside these ranges and needn't reach their ends.
Inputs may be any that keep to these rules, and one draw needn't show every extreme that they name: `node_map`: row c holds local node numbers of partition c // 4; the nodes of a cell are distinct and every local node belongs to some cell of its partition. `share_list`: row 0 of partition q lists its local nodes that are also nodes of partition q - 1, row 1 those that are also nodes of partition q + 1, cyclically; the k-th node of row 1 of q is the same node as the k-th node of row 0 of q + 1. Within a partition the two rows are disjoint and their entries distinct. `contacts`: column e belongs to partition e // 16: row 0 is a local cell number below 4, row 1 an atom; no pair of cell and atom repeats within a partition. Each partition is home to 4 atoms, and every entry of an atom lies in its home partition or in one of the two beside it, cyclically.
All inputs are finite; a program needn't handle non-finite values.
Results may differ from the reference program's by a relative error of at most 0.0003.
Values may be sent and summed in bfloat16 or wider, within the bound.
A program may use at most 64 MiB of HBM per device.

```python
import math
import jax
import jax.numpy as jnp
from jax import lax

BANDS = 192
DEGREE = 6
CELL_NODES = 343
CHAIN_CELLS = 1
CELLS_DEV = 4
FACE = 169
NODES_DEV = 1183
NODES = 9464
ATOM_DEV = 4
ATOMS = 32
NPROJ = 8
OVL_DEV = 16
OVL = 128
N_CELL = 8


def draw_cell_matrix(key, part):
    key_diag = jax.random.fold_in(key, 3)
    key_noise = jax.random.fold_in(key, 5)
    cell_total = N_CELL * CELLS_DEV
    diagonal_part = jnp.exp(jax.random.uniform(key_diag, (cell_total, CELL_NODES), jnp.float32, math.log(0.05), math.log(0.3)))
    noise_part = jax.random.normal(key_noise, (cell_total, CELL_NODES, CELL_NODES), jnp.float32)
    noise_part = (noise_part + jnp.swapaxes(noise_part, 1, 2)) * (0.01 / math.sqrt(2.0))
    return noise_part + diagonal_part[:, :, None] * jnp.eye(CELL_NODES, dtype=jnp.float32)[None]


def local_numbers(key):
    part_keys = jax.random.split(jax.random.fold_in(key, 11), N_CELL)
    return jax.vmap(lambda one_key: jax.random.permutation(one_key, NODES_DEV))(part_keys).astype(jnp.int32)


def draw_node_map(key, part):
    numbers = local_numbers(key)
    side_nodes = 2 * DEGREE + 1
    edge_nodes = DEGREE + 1
    cell_ids = jnp.arange(CELLS_DEV, dtype=jnp.int32)
    node_ids = jnp.arange(CELL_NODES, dtype=jnp.int32)
    cell_level = cell_ids // 4
    cell_line = cell_ids // 2 % 2
    cell_place = cell_ids % 2
    node_level = node_ids // (edge_nodes * edge_nodes)
    node_line = node_ids // edge_nodes % edge_nodes
    node_place = node_ids % edge_nodes
    canonical = ((cell_level[:, None] * DEGREE + node_level[None, :]) * side_nodes + cell_line[:, None] * DEGREE + node_line[None, :]) * side_nodes + cell_place[:, None] * DEGREE + node_place[None, :]
    return numbers[:, canonical].reshape(N_CELL * CELLS_DEV, CELL_NODES)


def draw_share_list(key, part):
    numbers = local_numbers(key)
    face_ids = jnp.arange(FACE, dtype=jnp.int32)
    top_ids = face_ids + CHAIN_CELLS * DEGREE * FACE
    return jnp.stack([numbers[:, face_ids], numbers[:, top_ids]], axis=1)


def draw_contacts(key, part):
    atom_order = jax.random.permutation(jax.random.fold_in(key, 23), ATOMS).astype(jnp.int32)
    part_keys = jax.random.split(jax.random.fold_in(key, 29), N_CELL)
    pair_total = 3 * ATOM_DEV * CELLS_DEV

    def part_entries(one_key, home_part):
        chosen = jax.random.permutation(one_key, pair_total)[:OVL_DEV].astype(jnp.int32)
        cell_pick = chosen % CELLS_DEV
        remains = chosen // CELLS_DEV
        offset_part = remains // ATOM_DEV - 1
        atom_slot = remains % ATOM_DEV
        atom_home = (home_part + offset_part) % N_CELL
        atom_ids = atom_order[atom_home * ATOM_DEV + atom_slot]
        return jnp.stack([cell_pick, atom_ids])
    entries = jax.vmap(part_entries)(part_keys, jnp.arange(N_CELL, dtype=jnp.int32))
    return entries.transpose(1, 0, 2).reshape(2, N_CELL * OVL_DEV)


def set_ends(values, key, low, top_value):
    spot = [jax.random.randint(jax.random.fold_in(key, axis), (), 0, length) for axis, length in enumerate(values.shape)]
    widest = values.shape.index(max(values.shape))
    beside = spot[:widest] + [(spot[widest] + 1) % values.shape[widest]] + spot[widest + 1:]
    return values.at[tuple(spot)].set(low).at[tuple(beside)].set(top_value)


def block_levels(rng, dims, pieces, least, top_value):
    def one(dim, blocks):
        steps = jax.random.uniform(jax.random.fold_in(jax.random.fold_in(rng, 6), dim), (blocks,), jnp.float32, least / len(pieces), top_value / len(pieces))
        return jnp.repeat(jnp.exp(steps), dims[dim] // blocks).reshape((-1,) + (1,) * (len(dims) - dim - 1))

    factor_of = one(*pieces[0])
    for cut in pieces[1:]:
        factor_of = factor_of * one(*cut)
    return factor_of


def gaussian(rng, shape, width, limit, cuts=(), kind=jnp.bfloat16):
    gain = block_levels(rng, shape, cuts, -0.22, 0.18) if cuts else 1.0
    result = jax.random.normal(rng, shape, jnp.float32) * width * gain
    return jnp.minimum(jnp.maximum(result, -limit), limit).astype(kind)


def setup_inputs(seed: int = 0) -> dict:
    arg_keys = jax.random.split(jax.random.key(seed), 10)
    return {
        "waves": gaussian(arg_keys[0], (BANDS, NODES), 1.0, 6.0, ((0, 4), (1, 8)), jnp.float32),
        "cell_matrix": draw_cell_matrix(jax.random.fold_in(arg_keys[9], 71), 0),
        "node_map": draw_node_map(jax.random.fold_in(arg_keys[9], 71), 0),
        "share_list": draw_share_list(jax.random.fold_in(arg_keys[9], 71), 0),
        "contacts": draw_contacts(jax.random.fold_in(arg_keys[9], 71), 0),
        "proj_values": gaussian(arg_keys[5], (OVL, NPROJ, CELL_NODES), CELL_NODES ** -0.5, 0.3125, ((0, 8),), jnp.float32),
        "coupling": jnp.clip(jax.random.uniform(arg_keys[6], (ATOMS, NPROJ), jnp.float32, -1.0, 1.0), -1.0, 1.0),
        "proj_count": set_ends(jax.random.randint(arg_keys[7], (ATOMS,), 1, NPROJ + 1), jax.random.fold_in(arg_keys[7], 1), 1, NPROJ).astype(jnp.int32),
        "mass": jnp.clip(jnp.exp(math.log(2.0) - 1.3862944 * jax.random.uniform(arg_keys[8], (NODES,), jnp.float32) ** block_levels(arg_keys[8], (NODES,), ((0, 8),), -0.2, 0.2)), 0.5, 2.0),
    }


PRECISE = lax.Precision.HIGHEST
CENTER = 1.0
HALF_WIDTH = 1.0
LOWEST = -0.5

def filter_terms():
    sigma_now = HALF_WIDTH / (LOWEST - CENTER)
    gamma_ratio = 2.0 / sigma_now
    first_scale = sigma_now / HALF_WIDTH
    later_terms = []
    for turn_index in range(2):
        sigma_next = 1.0 / (gamma_ratio - sigma_now)
        later_terms.append((2.0 * sigma_next / HALF_WIDTH, sigma_now * sigma_next))
        sigma_now = sigma_next
    return (first_scale, later_terms)

def atom_partials(values, part_nodes, part_over, part_proj):
    cell_vals = values[:, part_nodes]
    entry_vals = cell_vals[:, part_over[0], :]
    coeffs = jnp.einsum('bei,epi->bep', entry_vals, part_proj, precision=PRECISE)
    onehot_atom = (part_over[1][:, None] == jnp.arange(ATOMS, dtype=jnp.int32)[None, :]).astype(jnp.float32)
    return jnp.einsum('bep,ea->bap', coeffs, onehot_atom, precision=PRECISE)

def assemble_part(values, part_matrix, part_nodes, part_over, part_proj, scaled):
    cell_vals = values[:, part_nodes]
    cell_out = jnp.einsum('bcj,cij->bci', cell_vals, part_matrix, precision=PRECISE)
    onehot_atom = (part_over[1][:, None] == jnp.arange(ATOMS, dtype=jnp.int32)[None, :]).astype(jnp.float32)
    onehot_cell = (part_over[0][:, None] == jnp.arange(CELLS_DEV, dtype=jnp.int32)[None, :]).astype(jnp.float32)
    returned = jnp.einsum('bap,ea->bep', scaled, onehot_atom, precision=PRECISE)
    added_terms = jnp.einsum('bep,epi->bei', returned, part_proj, precision=PRECISE)
    cell_out = cell_out + jnp.einsum('bei,ec->bci', added_terms, onehot_cell, precision=PRECISE)
    return jnp.zeros((BANDS, NODES_DEV), jnp.float32).at[:, part_nodes].add(cell_out)

def take_columns(part_block, node_index):
    return part_block[:, node_index]

def add_faces(part_block, low_index, high_index, low_add, high_add):
    return part_block.at[:, low_index].add(low_add).at[:, high_index].add(high_add)

def reference(waves, cell_matrix, node_map, share_list, contacts, proj_values, coupling, proj_count, mass):
    part_waves = waves.reshape(BANDS, N_CELL, NODES_DEV).transpose(1, 0, 2)
    part_matrix = cell_matrix.reshape(N_CELL, CELLS_DEV, CELL_NODES, CELL_NODES)
    part_nodes = node_map.reshape(N_CELL, CELLS_DEV, CELL_NODES)
    part_over = contacts.reshape(2, N_CELL, OVL_DEV).transpose(1, 0, 2)
    part_proj = proj_values.reshape(N_CELL, OVL_DEV, NPROJ, CELL_NODES)
    part_mass = mass.reshape(N_CELL, NODES_DEV)
    levels = jnp.arange(NPROJ, dtype=jnp.int32)
    scales = coupling * (levels[None, :] < proj_count[:, None]).astype(jnp.float32)

    def apply_operator(values):

        def add_table(running, part_items):
            return (running + atom_partials(part_items[0], part_items[1], part_items[2], part_items[3]), None)
        summed, unused = lax.scan(add_table, jnp.zeros((BANDS, ATOMS, NPROJ), jnp.float32), (values, part_nodes, part_over, part_proj))
        scaled = summed * scales[None]
        assembled = lax.map(lambda part_items: assemble_part(part_items[0], part_items[1], part_items[2], part_items[3], part_items[4], scaled), (values, part_matrix, part_nodes, part_over, part_proj))
        low_faces = jax.vmap(take_columns)(assembled, share_list[:, 0])
        high_faces = jax.vmap(take_columns)(assembled, share_list[:, 1])
        from_prev = jnp.roll(high_faces, 1, axis=0)
        from_next = jnp.roll(low_faces, -1, axis=0)
        return jax.vmap(add_faces)(assembled, share_list[:, 0], share_list[:, 1], from_prev, from_next)
    first_scale, later_terms = filter_terms()
    previous = part_waves
    current = first_scale * (apply_operator(previous) - CENTER * previous)
    for lead_scale, back_scale in later_terms:
        upcoming = lead_scale * (apply_operator(current) - CENTER * current) - back_scale * previous
        previous, current = (current, upcoming)
    owned = jax.vmap(lambda node_index: jnp.ones((NODES_DEV,), jnp.float32).at[node_index].set(0.0))(share_list[:, 0])
    zed = (current * (owned * jnp.sqrt(part_mass))[:, None, :]).astype(jnp.bfloat16)

    def add_gram(running, zed_part):
        return (running + jnp.dot(zed_part, zed_part.T, preferred_element_type=jnp.float32), None)
    summed_gram, unused = lax.scan(add_gram, jnp.zeros((BANDS, BANDS), jnp.float32), zed)
    gram = summed_gram / math.sqrt(N_CELL * NODES_DEV)
    band_ids = jnp.arange(BANDS, dtype=jnp.int32)
    gram = jnp.where(band_ids[:, None] == band_ids[None, :], 0.0, gram)
    filtered = current.transpose(1, 0, 2).reshape(BANDS, N_CELL * NODES_DEV)
    return (filtered, gram)
```

```python
import functools
import math

import jax
import jax.numpy as jnp
from jax import lax
from jax.experimental import pallas as pl
from jax.experimental.pallas import tpu as pltpu
from jax.sharding import PartitionSpec as P

CENTER = 1.0
HALF_WIDTH = 1.0
LOWEST = -0.5
MESH = pl.DeviceIdType.MESH
F32 = jnp.float32
BF16 = jnp.bfloat16
NN = (((1,), (0,)), ((), ()))
NT = (((1,), (1,)), ((), ()))


def filter_terms():
    sigma_now = HALF_WIDTH / (LOWEST - CENTER)
    gamma_ratio = 2.0 / sigma_now
    terms = [(sigma_now / HALF_WIDTH, 0.0)]
    for turn_index in range(2):
        sigma_next = 1.0 / (gamma_ratio - sigma_now)
        terms.append((2.0 * sigma_next / HALF_WIDTH, sigma_now * sigma_next))
        sigma_now = sigma_next
    return terms


def up(size, unit):
    return -(-size // unit) * unit


def mm(left, right, dims):
    return lax.dot_general(left, right, dims, preferred_element_type=F32)


def halves(value):
    high = value.astype(BF16)
    low = (value - high.astype(F32)).astype(BF16)
    return high, low


def split_rows(value):
    return jnp.concatenate(halves(value), axis=0)


def join_rows(value):
    rows = value.shape[0] // 2
    return value[:rows] + value[rows:]


def iota(shape, axis):
    return lax.broadcasted_iota(jnp.int32, shape, axis)


def as_column(row):
    size = row.shape[1]
    eye = iota((size, size), 0) == iota((size, size), 1)
    return jnp.sum(jnp.where(eye, row, 0.0), axis=1, keepdims=True)


def as_row(column):
    size = column.shape[0]
    eye = iota((size, size), 0) == iota((size, size), 1)
    return jnp.sum(jnp.where(eye, column, 0.0), axis=0, keepdims=True)


def one_hot(mask):
    return jnp.where(mask, 1.0, 0.0).astype(BF16)


OFFSETS = (1, -1, 2, -2)


def kernel(
    n_cell,
    n_band,
    waves,
    cell_matrix,
    node_map,
    share_list,
    contacts,
    proj_values,
    coupling,
    proj_count,
    mass,
    filtered,
    gram,
    spots,
    pairs,
    lanes_of,
    faces_of,
    face_spot,
    projs,
    proj_node,
    mixed,
    vals,
    sums,
    y0,
    y1,
    y2,
    ids,
    near_ids,
    coeff_own,
    coeff_near,
    face_send,
    face_recv,
    zeds,
    grams,
    id_sems,
    coeff_sems,
    face_sems,
    zed_sems,
    gram_sems,
):
    me = lax.axis_index("cell")
    group = lax.axis_index("band")
    bands, nodes = waves.shape
    cells, cell_nodes = node_map.shape
    face = share_list.shape[1]
    entries, slots, _ = proj_values.shape
    terms = entries * slots
    atoms = coupling.shape[0]
    node_pad = y0.shape[1]
    cell_pad = lanes_of.shape[1]
    face_pad = faces_of.shape[1]

    def peer(offset):
        return {"cell": lax.rem(me + (offset + n_cell), n_cell)}

    def band_peer(offset):
        return {"band": lax.rem(group + offset, n_band)}

    barrier = pltpu.get_barrier_semaphore()
    for offset in range(1, n_cell):
        pl.semaphore_signal(barrier, inc=1, device_id=peer(offset), device_id_type=MESH)
    for offset in range(1, n_band):
        pl.semaphore_signal(barrier, inc=1, device_id=band_peer(offset), device_id_type=MESH)

    pick = iota((terms, entries), 0) // slots == iota((terms, entries), 1)
    held = contacts[...].astype(F32)
    cell_col = jnp.sum(jnp.where(pick, held[0:1], 0.0), axis=1, keepdims=True)
    atom_col = jnp.sum(jnp.where(pick, held[1:2], 0.0), axis=1, keepdims=True)
    slot_col = (iota((terms, 1), 0) % slots).astype(F32)
    id_col = atom_col * slots + slot_col
    ids[...] = jnp.broadcast_to(as_row(id_col), ids.shape)

    pl.semaphore_wait(barrier, n_cell - 1 + n_band - 1)
    started = []
    for k, offset in enumerate(OFFSETS):
        copy = pltpu.make_async_remote_copy(
            ids, near_ids.at[k], id_sems.at[0, k], id_sems.at[1, k],
            device_id=peer(offset), device_id_type=MESH,
        )
        copy.start()
        started.append(copy)

    count_col = as_column(proj_count[...].astype(F32))
    kept = iota((atoms, slots), 1).astype(F32) < count_col
    scales = jnp.where(kept, coupling[...], 0.0)
    atom_hot = jnp.where(atom_col == iota((terms, atoms), 1).astype(F32), 1.0, 0.0)
    scale_all = lax.dot_general(
        atom_hot, scales, NN, precision=lax.Precision.HIGHEST, preferred_element_type=F32
    )
    own_slot = iota((terms, slots), 1).astype(F32) == slot_col
    scale_row = as_row(jnp.sum(jnp.where(own_slot, scale_all, 0.0), axis=1, keepdims=True))

    lanes_of[...] = jnp.full(lanes_of.shape, -1, jnp.int32)
    lanes_of[:, :cell_nodes] = node_map[...]
    faces_of[...] = jnp.full(faces_of.shape, -2, jnp.int32)
    faces_of[:, :face] = share_list[...]
    for c in range(cells):
        spots[:, c * cell_pad : (c + 1) * cell_pad] = one_hot(
            iota((node_pad, cell_pad), 0) == lanes_of[c : c + 1, :]
        )
    for side in range(2):
        face_row = faces_of[side : side + 1, :]
        face_col = as_column(face_row.astype(F32)).astype(jnp.int32)
        here = slice(side * face_pad, (side + 1) * face_pad)
        face_spot[:, here] = one_hot(iota((node_pad, face_pad), 0) == face_row)
        for c in range(cells):
            pairs[here, c * cell_pad : (c + 1) * cell_pad] = one_hot(
                face_col == lanes_of[c : c + 1, :]
            )

    projs[...] = jnp.zeros(projs.shape, BF16)
    flat_high, flat_low = halves(proj_values[...].reshape(terms, cell_nodes))
    for c in range(cells):
        lanes = slice(c * cell_pad, c * cell_pad + cell_nodes)
        inside = cell_col == float(c)
        projs[0:terms, lanes] = jnp.where(inside, flat_high.astype(F32), 0.0).astype(BF16)
        projs[terms : 2 * terms, lanes] = jnp.where(inside, flat_low.astype(F32), 0.0).astype(BF16)
    proj_node[...] = mm(projs[...], spots[...], NT).astype(BF16)

    mixed[...] = jnp.zeros(mixed.shape, BF16)
    for c in range(cells):
        high, low = halves(cell_matrix[c])
        mixed[c, 0:cell_nodes, 0:cell_nodes] = high
        mixed[c, cell_pad : cell_pad + cell_nodes, 0:cell_nodes] = low

    y0[...] = jnp.zeros(y0.shape, F32)
    y0[:, :nodes] = waves[...]

    for copy in started:
        copy.wait()
    sums[:, 0:terms] = one_hot(id_col == ids[0:1, :])
    for k in range(len(OFFSETS)):
        sums[:, (k + 1) * terms : (k + 2) * terms] = one_hot(id_col == near_ids[k, 0:1, :])

    previous, current = None, y0[...]
    for turn, (lead, back) in enumerate(filter_terms()):
        values = split_rows(current)
        product = mm(values, proj_node[...], NT)
        product = join_rows(product)
        coeff_own[turn] = product[:, :terms] + product[:, terms:]
        coeff_copies = []
        for k, offset in enumerate(OFFSETS):
            copy = pltpu.make_async_remote_copy(
                coeff_own.at[turn], coeff_near.at[turn, k],
                coeff_sems.at[0, turn, k], coeff_sems.at[1, turn, k],
                device_id=peer(offset), device_id_type=MESH,
            )
            copy.start()
            coeff_copies.append(copy)

        gathered = mm(values, spots[...], NN).astype(BF16)
        for c in range(cells):
            lanes = slice(c * cell_pad, (c + 1) * cell_pad)
            product = join_rows(mm(gathered[:, lanes], mixed[c], NT))
            vals[:, lanes] = product[:, :cell_pad] + product[:, cell_pad:]

        for copy in coeff_copies:
            copy.wait()
        near = jnp.concatenate(
            [coeff_own[turn]] + [coeff_near[turn, k] for k in range(len(OFFSETS))], axis=1
        )
        scaled = split_rows(join_rows(mm(split_rows(near), sums[...], NT)) * scale_row)
        added = mm(jnp.concatenate([scaled, scaled], axis=1), projs[...], NN)
        cell_out = split_rows(vals[...] + join_rows(added))

        face_vals = join_rows(mm(cell_out, pairs[...], NT))
        face_copies = []
        for side in range(2):
            face_send[turn, side] = face_vals[:, side * face_pad : (side + 1) * face_pad]
            copy = pltpu.make_async_remote_copy(
                face_send.at[turn, side], face_recv.at[turn, 1 - side],
                face_sems.at[0, turn, side], face_sems.at[1, turn, side],
                device_id=peer(2 * side - 1), device_id_type=MESH,
            )
            copy.start()
            face_copies.append(copy)
        assembled = join_rows(mm(cell_out, spots[...], NT))
        assembled = lead * (assembled - CENTER * current)
        if previous is not None:
            assembled = assembled - back * previous
        for copy in face_copies:
            copy.wait()
        arrived = jnp.concatenate([face_recv[turn, 0], face_recv[turn, 1]], axis=1)
        arrived = join_rows(mm(split_rows(arrived), face_spot[...], NT))
        held_ref = (y1, y2, y1)[turn]
        previous = current
        held_ref[...] = assembled + lead * arrived
        current = held_ref[...]

    filtered[...] = current[:, :nodes]
    shared = mm(jnp.ones((16, face_pad), BF16), face_spot[:, 0:face_pad], NT)[0:1]
    y0[...] = jnp.zeros(y0.shape, F32)
    y0[0:1, :nodes] = jnp.sqrt(mass[...])
    weight = (1.0 - shared) * y0[0:1, :]
    zeds[group] = (current * weight).astype(BF16)
    copies = []
    for offset in range(1, n_band):
        copy = pltpu.make_async_remote_copy(
            zeds.at[group], zeds.at[group], zed_sems.at[0, offset - 1], zed_sems.at[1, offset - 1],
            device_id=band_peer(offset), device_id_type=MESH,
        )
        copy.start()
        copies.append(copy)
    for copy in copies:
        copy.wait_recv()
    grams[me] = mm(zeds[group], zeds[...].reshape(n_band * bands, node_pad), NT)
    for offset in range(1, n_cell):
        copy = pltpu.make_async_remote_copy(
            grams.at[me], grams.at[me], gram_sems.at[0, offset - 1], gram_sems.at[1, offset - 1],
            device_id=peer(offset), device_id_type=MESH,
        )
        copy.start()
        copies.append(copy)
    for copy in copies[n_band - 1 :]:
        copy.wait_recv()
    total = grams[0]
    for part in range(1, n_cell):
        total = total + grams[part]
    total = total / math.sqrt(n_cell * nodes)
    rows = group * bands + iota(total.shape, 0)
    gram[...] = jnp.where(rows == iota(total.shape, 1), 0.0, total)
    for copy in copies:
        copy.wait_send()


def on_device(
    waves, cell_matrix, node_map, share_list, contacts, proj_values, coupling, proj_count, mass
):
    n_cell = lax.axis_size("cell")
    n_band = lax.axis_size("band")
    bands, nodes = waves.shape
    cells, cell_nodes = node_map.shape
    entries, slots, _ = proj_values.shape
    terms = entries * slots
    node_pad = up(nodes, 128)
    cell_pad = up(cell_nodes, 128)
    face_pad = up(share_list.shape[2], 128)
    wide = cells * cell_pad
    peers = len(OFFSETS)
    dma = pltpu.SemaphoreType.DMA
    return pl.pallas_call(
        functools.partial(kernel, n_cell, n_band),
        out_shape=(
            jax.ShapeDtypeStruct((bands, nodes), F32),
            jax.ShapeDtypeStruct((bands, n_band * bands), F32),
        ),
        in_specs=[pl.BlockSpec(memory_space=pltpu.VMEM)] * 9,
        out_specs=(pl.BlockSpec(memory_space=pltpu.VMEM),) * 2,
        scratch_shapes=[
            pltpu.VMEM((node_pad, wide), BF16),
            pltpu.VMEM((2 * face_pad, wide), BF16),
            pltpu.VMEM((cells, cell_pad), jnp.int32),
            pltpu.VMEM((2, face_pad), jnp.int32),
            pltpu.VMEM((node_pad, 2 * face_pad), BF16),
            pltpu.VMEM((2 * terms, wide), BF16),
            pltpu.VMEM((2 * terms, node_pad), BF16),
            pltpu.VMEM((cells, 2 * cell_pad, cell_pad), BF16),
            pltpu.VMEM((bands, wide), F32),
            pltpu.VMEM((terms, (1 + peers) * terms), BF16),
            pltpu.VMEM((bands, node_pad), F32),
            pltpu.VMEM((bands, node_pad), F32),
            pltpu.VMEM((bands, node_pad), F32),
            pltpu.VMEM((8, terms), F32),
            pltpu.VMEM((peers, 8, terms), F32),
            pltpu.VMEM((3, bands, terms), F32),
            pltpu.VMEM((3, peers, bands, terms), F32),
            pltpu.VMEM((3, 2, bands, face_pad), F32),
            pltpu.VMEM((3, 2, bands, face_pad), F32),
            pltpu.VMEM((n_band, bands, node_pad), BF16),
            pltpu.VMEM((n_cell, bands, n_band * bands), F32),
            dma((2, peers)),
            dma((2, 3, peers)),
            dma((2, 3, 2)),
            dma((2, n_band - 1)),
            dma((2, n_cell - 1)),
        ],
        compiler_params=pltpu.CompilerParams(
            collective_id=0, has_side_effects=True, vmem_limit_bytes=48 * 1024 * 1024
        ),
    )(
        waves,
        cell_matrix,
        node_map,
        share_list.reshape(share_list.shape[1:]),
        contacts,
        proj_values,
        coupling,
        proj_count.reshape(1, -1),
        mass.reshape(1, -1),
    )


def solution(mesh):
    return jax.shard_map(
        on_device,
        mesh=mesh,
        in_specs=(
            P("band", "cell"),
            P("cell", None, None),
            P("cell", None),
            P("cell", None, None),
            P(None, "cell"),
            P("cell", None, None),
            P(),
            P(),
            P("cell"),
        ),
        out_specs=(P("band", "cell"), P("band", None)),
        check_vma=False,
    )
```

```python
import functools
import math

import jax
import jax.numpy as jnp
from jax import lax
from jax.experimental import pallas as pl
from jax.experimental.pallas import tpu as pltpu
from jax.sharding import PartitionSpec as P

CENTER = 1.0
HALF_WIDTH = 1.0
LOWEST = -0.5
MESH = pl.DeviceIdType.MESH
F32 = jnp.float32
BF16 = jnp.bfloat16
NN = (((1,), (0,)), ((), ()))
NT = (((1,), (1,)), ((), ()))


def filter_terms():
    sigma_now = HALF_WIDTH / (LOWEST - CENTER)
    gamma_ratio = 2.0 / sigma_now
    terms = [(sigma_now / HALF_WIDTH, 0.0)]
    for turn_index in range(2):
        sigma_next = 1.0 / (gamma_ratio - sigma_now)
        terms.append((2.0 * sigma_next / HALF_WIDTH, sigma_now * sigma_next))
        sigma_now = sigma_next
    return terms


def up(size, unit):
    return -(-size // unit) * unit


def mm(left, right, dims):
    return lax.dot_general(left, right, dims, preferred_element_type=F32)


def halves(value):
    high = value.astype(BF16)
    low = (value - high.astype(F32)).astype(BF16)
    return high, low


def split_rows(value):
    return jnp.concatenate(halves(value), axis=0)


def join_rows(value):
    rows = value.shape[0] // 2
    return value[:rows] + value[rows:]


def iota(shape, axis):
    return lax.broadcasted_iota(jnp.int32, shape, axis)


def as_column(row):
    size = row.shape[1]
    eye = iota((size, size), 0) == iota((size, size), 1)
    return jnp.sum(jnp.where(eye, row, 0.0), axis=1, keepdims=True)


def as_row(column):
    size = column.shape[0]
    eye = iota((size, size), 0) == iota((size, size), 1)
    return jnp.sum(jnp.where(eye, column, 0.0), axis=0, keepdims=True)


def one_hot(mask):
    return jnp.where(mask, 1.0, 0.0).astype(BF16)


OFFSETS = (1, -1, 2, -2)


def kernel(
    n_cell,
    n_band,
    waves,
    cell_matrix,
    node_map,
    share_list,
    contacts,
    proj_values,
    coupling,
    proj_count,
    mass,
    filtered,
    gram,
    spots,
    pairs,
    lanes_of,
    faces_of,
    face_spot,
    projs,
    proj_node,
    mixed,
    vals,
    sums,
    y0,
    y1,
    y2,
    ids,
    near_ids,
    coeff_own,
    coeff_near,
    face_send,
    face_recv,
    zed_half,
    zeds,
    block_send,
    block_recv,
    grams,
    id_sems,
    coeff_sems,
    face_sems,
    zed_sems,
    block_sems,
    gram_sems,
):
    me = lax.axis_index("cell")
    group = lax.axis_index("band")
    bands, nodes = waves.shape
    cells, cell_nodes = node_map.shape
    face = share_list.shape[1]
    entries, slots, _ = proj_values.shape
    terms = entries * slots
    atoms = coupling.shape[0]
    node_pad = y0.shape[1]
    cell_pad = lanes_of.shape[1]
    face_pad = faces_of.shape[1]

    def peer(offset):
        return {"cell": lax.rem(me + (offset + n_cell), n_cell)}

    def band_peer(offset):
        return {"band": lax.rem(group + offset, n_band)}

    barrier = pltpu.get_barrier_semaphore()
    for offset in range(1, n_cell):
        pl.semaphore_signal(barrier, inc=1, device_id=peer(offset), device_id_type=MESH)
    for offset in range(1, n_band):
        pl.semaphore_signal(barrier, inc=1, device_id=band_peer(offset), device_id_type=MESH)

    pick = iota((terms, entries), 0) // slots == iota((terms, entries), 1)
    held = contacts[...].astype(F32)
    cell_col = jnp.sum(jnp.where(pick, held[0:1], 0.0), axis=1, keepdims=True)
    atom_col = jnp.sum(jnp.where(pick, held[1:2], 0.0), axis=1, keepdims=True)
    slot_col = (iota((terms, 1), 0) % slots).astype(F32)
    id_col = atom_col * slots + slot_col
    ids[...] = jnp.broadcast_to(as_row(id_col), ids.shape)

    pl.semaphore_wait(barrier, n_cell - 1 + n_band - 1)
    started = []
    for k, offset in enumerate(OFFSETS):
        copy = pltpu.make_async_remote_copy(
            ids, near_ids.at[k], id_sems.at[0, k], id_sems.at[1, k],
            device_id=peer(offset), device_id_type=MESH,
        )
        copy.start()
        started.append(copy)

    count_col = as_column(proj_count[...].astype(F32))
    kept = iota((atoms, slots), 1).astype(F32) < count_col
    scales = jnp.where(kept, coupling[...], 0.0)
    atom_hot = jnp.where(atom_col == iota((terms, atoms), 1).astype(F32), 1.0, 0.0)
    scale_all = lax.dot_general(
        atom_hot, scales, NN, precision=lax.Precision.HIGHEST, preferred_element_type=F32
    )
    own_slot = iota((terms, slots), 1).astype(F32) == slot_col
    scale_row = as_row(jnp.sum(jnp.where(own_slot, scale_all, 0.0), axis=1, keepdims=True))

    lanes_of[...] = jnp.full(lanes_of.shape, -1, jnp.int32)
    lanes_of[:, :cell_nodes] = node_map[...]
    faces_of[...] = jnp.full(faces_of.shape, -2, jnp.int32)
    faces_of[:, :face] = share_list[...]
    for c in range(cells):
        spots[:, c * cell_pad : (c + 1) * cell_pad] = one_hot(
            iota((node_pad, cell_pad), 0) == lanes_of[c : c + 1, :]
        )
    for side in range(2):
        face_row = faces_of[side : side + 1, :]
        face_col = as_column(face_row.astype(F32)).astype(jnp.int32)
        here = slice(side * face_pad, (side + 1) * face_pad)
        face_spot[:, here] = one_hot(iota((node_pad, face_pad), 0) == face_row)
        for c in range(cells):
            pairs[here, c * cell_pad : (c + 1) * cell_pad] = one_hot(
                face_col == lanes_of[c : c + 1, :]
            )

    projs[...] = jnp.zeros(projs.shape, BF16)
    flat_high, flat_low = halves(proj_values[...].reshape(terms, cell_nodes))
    for c in range(cells):
        lanes = slice(c * cell_pad, c * cell_pad + cell_nodes)
        inside = cell_col == float(c)
        projs[0:terms, lanes] = jnp.where(inside, flat_high.astype(F32), 0.0).astype(BF16)
        projs[terms : 2 * terms, lanes] = jnp.where(inside, flat_low.astype(F32), 0.0).astype(BF16)
    proj_node[...] = mm(projs[...], spots[...], NT).astype(BF16)

    mixed[...] = jnp.zeros(mixed.shape, BF16)
    for c in range(cells):
        high, low = halves(cell_matrix[c])
        mixed[c, 0:cell_nodes, 0:cell_nodes] = high
        mixed[c, cell_pad : cell_pad + cell_nodes, 0:cell_nodes] = low

    y0[...] = jnp.zeros(y0.shape, F32)
    y0[:, :nodes] = waves[...]

    for copy in started:
        copy.wait()
    sums[:, 0:terms] = one_hot(id_col == ids[0:1, :])
    for k in range(len(OFFSETS)):
        sums[:, (k + 1) * terms : (k + 2) * terms] = one_hot(id_col == near_ids[k, 0:1, :])

    previous, current = None, y0[...]
    for turn, (lead, back) in enumerate(filter_terms()):
        values = split_rows(current)
        product = mm(values, proj_node[...], NT)
        product = join_rows(product)
        coeff_own[turn] = product[:, :terms] + product[:, terms:]
        coeff_copies = []
        for k, offset in enumerate(OFFSETS):
            copy = pltpu.make_async_remote_copy(
                coeff_own.at[turn], coeff_near.at[turn, k],
                coeff_sems.at[0, turn, k], coeff_sems.at[1, turn, k],
                device_id=peer(offset), device_id_type=MESH,
            )
            copy.start()
            coeff_copies.append(copy)

        gathered = mm(values, spots[...], NN).astype(BF16)
        for c in range(cells):
            lanes = slice(c * cell_pad, (c + 1) * cell_pad)
            product = join_rows(mm(gathered[:, lanes], mixed[c], NT))
            vals[:, lanes] = product[:, :cell_pad] + product[:, cell_pad:]

        for copy in coeff_copies:
            copy.wait()
        near = jnp.concatenate(
            [coeff_own[turn]] + [coeff_near[turn, k] for k in range(len(OFFSETS))], axis=1
        )
        scaled = split_rows(join_rows(mm(split_rows(near), sums[...], NT)) * scale_row)
        added = mm(jnp.concatenate([scaled, scaled], axis=1), projs[...], NN)
        cell_out = split_rows(vals[...] + join_rows(added))

        face_vals = join_rows(mm(cell_out, pairs[...], NT))
        face_copies = []
        for side in range(2):
            face_send[turn, side] = face_vals[:, side * face_pad : (side + 1) * face_pad]
            copy = pltpu.make_async_remote_copy(
                face_send.at[turn, side], face_recv.at[turn, 1 - side],
                face_sems.at[0, turn, side], face_sems.at[1, turn, side],
                device_id=peer(2 * side - 1), device_id_type=MESH,
            )
            copy.start()
            face_copies.append(copy)
        assembled = join_rows(mm(cell_out, spots[...], NT))
        assembled = lead * (assembled - CENTER * current)
        if previous is not None:
            assembled = assembled - back * previous
        for copy in face_copies:
            copy.wait()
        arrived = jnp.concatenate([face_recv[turn, 0], face_recv[turn, 1]], axis=1)
        arrived = join_rows(mm(split_rows(arrived), face_spot[...], NT))
        held_ref = (y1, y2, y1)[turn]
        previous = current
        held_ref[...] = assembled + lead * arrived
        current = held_ref[...]

    filtered[...] = current[:, :nodes]
    shared = mm(jnp.ones((16, face_pad), BF16), face_spot[:, 0:face_pad], NT)[0:1]
    y0[...] = jnp.zeros(y0.shape, F32)
    y0[0:1, :nodes] = jnp.sqrt(mass[...])
    weight = (1.0 - shared) * y0[0:1, :]
    zed = (current * weight).astype(BF16)
    half = zed_half.shape[2]
    zed_half[0] = zed[:, :half]
    zed_half[1] = zed[:, half:]
    zeds[group] = zed[:, :half]
    copies = []
    for offset in range(1, n_band):
        copy = pltpu.make_async_remote_copy(
            zed_half.at[(group + offset) // n_band], zeds.at[group],
            zed_sems.at[0, offset - 1], zed_sems.at[1, offset - 1],
            device_id=band_peer(offset), device_id_type=MESH,
        )
        copy.start()
        copies.append(copy)
    own_block = mm(zed, zed, NT)
    for copy in copies:
        copy.wait_recv()
    others = zeds[...].reshape(n_band * bands, half)
    turned_first = mm(others, zed_half[0], NT)
    turned_second = mm(others, zed_half[1], NT)
    below = iota(turned_first.shape, 0) < group * bands
    block_send[...] = jnp.where(below, turned_first, turned_second).reshape(block_send.shape)
    block_copies = []
    for offset in range(1, n_band):
        copy = pltpu.make_async_remote_copy(
            block_send.at[lax.rem(group + offset, n_band)], block_recv.at[group],
            block_sems.at[0, offset - 1], block_sems.at[1, offset - 1],
            device_id=band_peer(offset), device_id_type=MESH,
        )
        copy.start()
        block_copies.append(copy)
    block_recv[group] = own_block
    straight_first = mm(zed_half[0], others, NT)
    straight_second = mm(zed_half[1], others, NT)
    places = iota(straight_first.shape, 1)
    straight = jnp.where(places < group * bands, straight_first, straight_second)
    inside = jnp.logical_and(places >= group * bands, places < (group + 1) * bands)
    straight = jnp.where(inside, 0.0, straight)
    for copy in block_copies:
        copy.wait()
    grams[me] = straight + jnp.concatenate([block_recv[j] for j in range(n_band)], axis=1)
    for offset in range(1, n_cell):
        copy = pltpu.make_async_remote_copy(
            grams.at[me], grams.at[me], gram_sems.at[0, offset - 1], gram_sems.at[1, offset - 1],
            device_id=peer(offset), device_id_type=MESH,
        )
        copy.start()
        copies.append(copy)
    for copy in copies[n_band - 1 :]:
        copy.wait_recv()
    total = grams[0]
    for part in range(1, n_cell):
        total = total + grams[part]
    total = total / math.sqrt(n_cell * nodes)
    rows = group * bands + iota(total.shape, 0)
    gram[...] = jnp.where(rows == iota(total.shape, 1), 0.0, total)
    for copy in copies:
        copy.wait_send()


def on_device(
    waves, cell_matrix, node_map, share_list, contacts, proj_values, coupling, proj_count, mass
):
    n_cell = lax.axis_size("cell")
    n_band = lax.axis_size("band")
    bands, nodes = waves.shape
    cells, cell_nodes = node_map.shape
    entries, slots, _ = proj_values.shape
    terms = entries * slots
    node_pad = up(nodes, 256)
    cell_pad = up(cell_nodes, 128)
    face_pad = up(share_list.shape[2], 128)
    wide = cells * cell_pad
    peers = len(OFFSETS)
    dma = pltpu.SemaphoreType.DMA
    return pl.pallas_call(
        functools.partial(kernel, n_cell, n_band),
        out_shape=(
            jax.ShapeDtypeStruct((bands, nodes), F32),
            jax.ShapeDtypeStruct((bands, n_band * bands), F32),
        ),
        in_specs=[pl.BlockSpec(memory_space=pltpu.VMEM)] * 9,
        out_specs=(pl.BlockSpec(memory_space=pltpu.VMEM),) * 2,
        scratch_shapes=[
            pltpu.VMEM((node_pad, wide), BF16),
            pltpu.VMEM((2 * face_pad, wide), BF16),
            pltpu.VMEM((cells, cell_pad), jnp.int32),
            pltpu.VMEM((2, face_pad), jnp.int32),
            pltpu.VMEM((node_pad, 2 * face_pad), BF16),
            pltpu.VMEM((2 * terms, wide), BF16),
            pltpu.VMEM((2 * terms, node_pad), BF16),
            pltpu.VMEM((cells, 2 * cell_pad, cell_pad), BF16),
            pltpu.VMEM((bands, wide), F32),
            pltpu.VMEM((terms, (1 + peers) * terms), BF16),
            pltpu.VMEM((bands, node_pad), F32),
            pltpu.VMEM((bands, node_pad), F32),
            pltpu.VMEM((bands, node_pad), F32),
            pltpu.VMEM((8, terms), F32),
            pltpu.VMEM((peers, 8, terms), F32),
            pltpu.VMEM((3, bands, terms), F32),
            pltpu.VMEM((3, peers, bands, terms), F32),
            pltpu.VMEM((3, 2, bands, face_pad), F32),
            pltpu.VMEM((3, 2, bands, face_pad), F32),
            pltpu.VMEM((2, bands, node_pad // 2), BF16),
            pltpu.VMEM((n_band, bands, node_pad // 2), BF16),
            pltpu.VMEM((n_band, bands, bands), F32),
            pltpu.VMEM((n_band, bands, bands), F32),
            pltpu.VMEM((n_cell, bands, n_band * bands), F32),
            dma((2, peers)),
            dma((2, 3, peers)),
            dma((2, 3, 2)),
            dma((2, n_band - 1)),
            dma((2, n_band - 1)),
            dma((2, n_cell - 1)),
        ],
        compiler_params=pltpu.CompilerParams(
            collective_id=0, has_side_effects=True, vmem_limit_bytes=48 * 1024 * 1024
        ),
    )(
        waves,
        cell_matrix,
        node_map,
        share_list.reshape(share_list.shape[1:]),
        contacts,
        proj_values,
        coupling,
        proj_count.reshape(1, -1),
        mass.reshape(1, -1),
    )


def solution(mesh):
    return jax.shard_map(
        on_device,
        mesh=mesh,
        in_specs=(
            P("band", "cell"),
            P("cell", None, None),
            P("cell", None),
            P("cell", None, None),
            P(None, "cell"),
            P("cell", None, None),
            P(),
            P(),
            P("cell"),
        ),
        out_specs=(P("band", "cell"), P("band", None)),
        check_vma=False,
    )
```

```python
import functools
import math

import jax
import jax.numpy as jnp
from jax import lax
from jax.experimental import pallas as pl
from jax.experimental.pallas import tpu as pltpu
from jax.sharding import PartitionSpec as P

CENTER = 1.0
HALF_WIDTH = 1.0
LOWEST = -0.5
MESH = pl.DeviceIdType.MESH
F32 = jnp.float32
BF16 = jnp.bfloat16
NN = (((1,), (0,)), ((), ()))
NT = (((1,), (1,)), ((), ()))


def filter_terms():
    sigma_now = HALF_WIDTH / (LOWEST - CENTER)
    gamma_ratio = 2.0 / sigma_now
    terms = [(sigma_now / HALF_WIDTH, 0.0)]
    for turn_index in range(2):
        sigma_next = 1.0 / (gamma_ratio - sigma_now)
        terms.append((2.0 * sigma_next / HALF_WIDTH, sigma_now * sigma_next))
        sigma_now = sigma_next
    return terms


def up(size, unit):
    return -(-size // unit) * unit


def mm(left, right, dims):
    return lax.dot_general(left, right, dims, preferred_element_type=F32)


def halves(value):
    high = value.astype(BF16)
    low = (value - high.astype(F32)).astype(BF16)
    return high, low


def split_rows(value):
    return jnp.concatenate(halves(value), axis=0)


def join_rows(value):
    rows = value.shape[0] // 2
    return value[:rows] + value[rows:]


def iota(shape, axis):
    return lax.broadcasted_iota(jnp.int32, shape, axis)


def as_column(row):
    size = row.shape[1]
    eye = iota((size, size), 0) == iota((size, size), 1)
    return jnp.sum(jnp.where(eye, row, 0.0), axis=1, keepdims=True)


def as_row(column):
    size = column.shape[0]
    eye = iota((size, size), 0) == iota((size, size), 1)
    return jnp.sum(jnp.where(eye, column, 0.0), axis=0, keepdims=True)


def one_hot(mask):
    return jnp.where(mask, 1.0, 0.0).astype(BF16)


OFFSETS = (1, -1, 2, -2)


def kernel(
    n_cell,
    n_band,
    waves,
    cell_matrix,
    node_map,
    share_list,
    contacts,
    proj_values,
    coupling,
    proj_count,
    mass,
    filtered,
    gram,
    spots,
    pairs,
    lanes_of,
    faces_of,
    face_spot,
    projs,
    proj_node,
    mixed,
    vals,
    sums,
    y0,
    y1,
    y2,
    roots,
    ids,
    near_ids,
    coeff_own,
    coeff_near,
    face_send,
    face_recv,
    zed_half,
    zeds,
    block_send,
    block_recv,
    grams,
    id_sems,
    coeff_sems,
    face_sems,
    zed_sems,
    block_sems,
    gram_sems,
):
    me = lax.axis_index("cell")
    group = lax.axis_index("band")
    bands, nodes = waves.shape
    cells, cell_nodes = node_map.shape
    face = share_list.shape[1]
    entries, slots, _ = proj_values.shape
    terms = entries * slots
    atoms = coupling.shape[1]
    node_pad = y0.shape[1]
    cell_pad = lanes_of.shape[1]
    face_pad = faces_of.shape[1]

    def peer(offset):
        return {"cell": lax.rem(me + (offset + n_cell), n_cell)}

    def band_peer(offset):
        return {"band": lax.rem(group + offset, n_band)}

    barrier = pltpu.get_barrier_semaphore()
    for offset in range(1, n_cell):
        pl.semaphore_signal(barrier, inc=1, device_id=peer(offset), device_id_type=MESH)
    for offset in range(1, n_band):
        pl.semaphore_signal(barrier, inc=1, device_id=band_peer(offset), device_id_type=MESH)

    pick = iota((terms, entries), 0) // slots == iota((terms, entries), 1)
    held = contacts[...].astype(F32)
    cell_col = jnp.sum(jnp.where(pick, held[0:1], 0.0), axis=1, keepdims=True)
    atom_col = jnp.sum(jnp.where(pick, held[1:2], 0.0), axis=1, keepdims=True)
    slot_col = (iota((terms, 1), 0) % slots).astype(F32)
    id_col = atom_col * slots + slot_col
    ids[...] = jnp.broadcast_to(as_row(id_col), ids.shape)

    pl.semaphore_wait(barrier, n_cell - 1 + n_band - 1)
    started = []
    for k, offset in enumerate(OFFSETS):
        copy = pltpu.make_async_remote_copy(
            ids, near_ids.at[k], id_sems.at[0, k], id_sems.at[1, k],
            device_id=peer(offset), device_id_type=MESH,
        )
        copy.start()
        started.append(copy)

    lanes_of[...] = jnp.full(lanes_of.shape, -1, jnp.int32)
    lanes_of[:, :cell_nodes] = node_map[...]
    faces_of[...] = jnp.full(faces_of.shape, -2, jnp.int32)
    faces_of[:, :face] = share_list[...]
    for c in range(cells):
        spots[:, c * cell_pad : (c + 1) * cell_pad] = one_hot(
            iota((node_pad, cell_pad), 0) == lanes_of[c : c + 1, :]
        )
    projs[...] = jnp.zeros(projs.shape, BF16)
    flat_high, flat_low = halves(proj_values[...].reshape(terms, cell_nodes))
    for c in range(cells):
        lanes = slice(c * cell_pad, c * cell_pad + cell_nodes)
        inside = cell_col == float(c)
        projs[0:terms, lanes] = jnp.where(inside, flat_high.astype(F32), 0.0).astype(BF16)
        projs[terms : 2 * terms, lanes] = jnp.where(inside, flat_low.astype(F32), 0.0).astype(BF16)
    proj_node[...] = mm(projs[...], spots[...], NT).astype(BF16)

    y0[...] = jnp.zeros(y0.shape, F32)
    y0[:, :nodes] = waves[...]

    previous, current = None, y0[...]
    for turn, (lead, back) in enumerate(filter_terms()):
        values = split_rows(current)
        product = mm(values, proj_node[...], NT)
        product = join_rows(product)
        coeff_own[turn] = product[:, :terms] + product[:, terms:]
        coeff_copies = []
        for k, offset in enumerate(OFFSETS):
            copy = pltpu.make_async_remote_copy(
                coeff_own.at[turn], coeff_near.at[turn, k],
                coeff_sems.at[0, turn, k], coeff_sems.at[1, turn, k],
                device_id=peer(offset), device_id_type=MESH,
            )
            copy.start()
            coeff_copies.append(copy)

        if turn == 0:
            mixed[...] = jnp.zeros(mixed.shape, BF16)
            for c in range(cells):
                high, low = halves(cell_matrix[c])
                mixed[c, 0:cell_nodes, 0:cell_nodes] = high
                mixed[c, cell_pad : cell_pad + cell_nodes, 0:cell_nodes] = low

            for side in range(2):
                face_row = faces_of[side : side + 1, :]
                face_col = as_column(face_row.astype(F32)).astype(jnp.int32)
                here = slice(side * face_pad, (side + 1) * face_pad)
                face_spot[:, here] = one_hot(iota((node_pad, face_pad), 0) == face_row)
                for c in range(cells):
                    pairs[here, c * cell_pad : (c + 1) * cell_pad] = one_hot(
                        face_col == lanes_of[c : c + 1, :]
                    )

            for copy in started:
                copy.wait()
            sums[:, 0:terms] = one_hot(id_col == ids[0:1, :])
            for k in range(len(OFFSETS)):
                sums[:, (k + 1) * terms : (k + 2) * terms] = one_hot(id_col == near_ids[k, 0:1, :])

            levels = iota((slots, atoms), 0)
            scales = jnp.where(levels < proj_count[...], coupling[...], 0.0)
            atom_hot = jnp.where(atom_col == iota((terms, atoms), 1).astype(F32), 1.0, 0.0)
            scale_all = lax.dot_general(
                atom_hot, scales, NT, precision=lax.Precision.HIGHEST, preferred_element_type=F32
            )
            own_slot = iota((terms, slots), 1).astype(F32) == slot_col
            scale_row = as_row(jnp.sum(jnp.where(own_slot, scale_all, 0.0), axis=1, keepdims=True))

            shared = mm(jnp.ones((16, face_pad), BF16), face_spot[:, 0:face_pad], NT)[0:1]
            roots[...] = jnp.zeros(roots.shape, F32)
            roots[:, :nodes] = jnp.sqrt(mass[...])
            weight_row = (1.0 - shared) * roots[...]
            roots[...] = weight_row

        gathered = mm(values, spots[...], NN).astype(BF16)
        for c in range(cells):
            lanes = slice(c * cell_pad, (c + 1) * cell_pad)
            product = join_rows(mm(gathered[:, lanes], mixed[c], NT))
            vals[:, lanes] = product[:, :cell_pad] + product[:, cell_pad:]

        for copy in coeff_copies:
            copy.wait()
        near = jnp.concatenate(
            [coeff_own[turn]] + [coeff_near[turn, k] for k in range(len(OFFSETS))], axis=1
        )
        scaled = split_rows(join_rows(mm(split_rows(near), sums[...], NT)) * scale_row)
        added = mm(jnp.concatenate([scaled, scaled], axis=1), projs[...], NN)
        cell_out = split_rows(vals[...] + join_rows(added))

        face_vals = join_rows(mm(cell_out, pairs[...], NT))
        face_copies = []
        for side in range(2):
            face_send[turn, side] = face_vals[:, side * face_pad : (side + 1) * face_pad]
            copy = pltpu.make_async_remote_copy(
                face_send.at[turn, side], face_recv.at[turn, 1 - side],
                face_sems.at[0, turn, side], face_sems.at[1, turn, side],
                device_id=peer(2 * side - 1), device_id_type=MESH,
            )
            copy.start()
            face_copies.append(copy)
        assembled = join_rows(mm(cell_out, spots[...], NT))
        assembled = lead * (assembled - CENTER * current)
        if previous is not None:
            assembled = assembled - back * previous
        for copy in face_copies:
            copy.wait()
        arrived = jnp.concatenate([face_recv[turn, 0], face_recv[turn, 1]], axis=1)
        arrived = join_rows(mm(split_rows(arrived), face_spot[...], NT))
        held_ref = (y1, y2, y1)[turn]
        previous = current
        held_ref[...] = assembled + lead * arrived
        current = held_ref[...]

    zed = (current * roots[...]).astype(BF16)
    half = zed_half.shape[2]
    zed_half[0] = zed[:, :half]
    zed_half[1] = zed[:, half:]
    zeds[group] = zed[:, :half]
    copies = []
    for offset in range(1, n_band):
        copy = pltpu.make_async_remote_copy(
            zed_half.at[(group + offset) // n_band], zeds.at[group],
            zed_sems.at[0, offset - 1], zed_sems.at[1, offset - 1],
            device_id=band_peer(offset), device_id_type=MESH,
        )
        copy.start()
        copies.append(copy)
    filtered[...] = current[:, :nodes]
    own_block = mm(zed, zed, NT)
    for copy in copies:
        copy.wait_recv()
    others = zeds[...].reshape(n_band * bands, half)
    turned_first = mm(others, zed_half[0], NT)
    turned_second = mm(others, zed_half[1], NT)
    below = iota(turned_first.shape, 0) < group * bands
    block_send[...] = jnp.where(below, turned_first, turned_second).reshape(block_send.shape)
    block_copies = []
    for offset in range(1, n_band):
        copy = pltpu.make_async_remote_copy(
            block_send.at[lax.rem(group + offset, n_band)], block_recv.at[group],
            block_sems.at[0, offset - 1], block_sems.at[1, offset - 1],
            device_id=band_peer(offset), device_id_type=MESH,
        )
        copy.start()
        block_copies.append(copy)
    block_recv[group] = own_block
    straight_first = mm(zed_half[0], others, NT)
    straight_second = mm(zed_half[1], others, NT)
    places = iota(straight_first.shape, 1)
    straight = jnp.where(places < group * bands, straight_first, straight_second)
    inside = jnp.logical_and(places >= group * bands, places < (group + 1) * bands)
    straight = jnp.where(inside, 0.0, straight)
    for copy in block_copies:
        copy.wait()
    grams[me] = straight + jnp.concatenate([block_recv[j] for j in range(n_band)], axis=1)
    for offset in range(1, n_cell):
        copy = pltpu.make_async_remote_copy(
            grams.at[me], grams.at[me], gram_sems.at[0, offset - 1], gram_sems.at[1, offset - 1],
            device_id=peer(offset), device_id_type=MESH,
        )
        copy.start()
        copies.append(copy)
    for copy in copies[n_band - 1 :]:
        copy.wait_recv()
    total = grams[0]
    for part in range(1, n_cell):
        total = total + grams[part]
    total = total / math.sqrt(n_cell * nodes)
    rows = group * bands + iota(total.shape, 0)
    gram[...] = jnp.where(rows == iota(total.shape, 1), 0.0, total)
    for copy in copies:
        copy.wait_send()


def on_device(
    waves, cell_matrix, node_map, share_list, contacts, proj_values, coupling, proj_count, mass
):
    n_cell = lax.axis_size("cell")
    n_band = lax.axis_size("band")
    bands, nodes = waves.shape
    cells, cell_nodes = node_map.shape
    entries, slots, _ = proj_values.shape
    terms = entries * slots
    node_pad = up(nodes, 256)
    cell_pad = up(cell_nodes, 128)
    face_pad = up(share_list.shape[2], 128)
    wide = cells * cell_pad
    peers = len(OFFSETS)
    dma = pltpu.SemaphoreType.DMA
    return pl.pallas_call(
        functools.partial(kernel, n_cell, n_band),
        out_shape=(
            jax.ShapeDtypeStruct((bands, nodes), F32),
            jax.ShapeDtypeStruct((bands, n_band * bands), F32),
        ),
        in_specs=[pl.BlockSpec(memory_space=pltpu.VMEM)] * 9,
        out_specs=(pl.BlockSpec(memory_space=pltpu.VMEM),) * 2,
        scratch_shapes=[
            pltpu.VMEM((node_pad, wide), BF16),
            pltpu.VMEM((2 * face_pad, wide), BF16),
            pltpu.VMEM((cells, cell_pad), jnp.int32),
            pltpu.VMEM((2, face_pad), jnp.int32),
            pltpu.VMEM((node_pad, 2 * face_pad), BF16),
            pltpu.VMEM((2 * terms, wide), BF16),
            pltpu.VMEM((2 * terms, node_pad), BF16),
            pltpu.VMEM((cells, 2 * cell_pad, cell_pad), BF16),
            pltpu.VMEM((bands, wide), F32),
            pltpu.VMEM((terms, (1 + peers) * terms), BF16),
            pltpu.VMEM((bands, node_pad), F32),
            pltpu.VMEM((bands, node_pad), F32),
            pltpu.VMEM((bands, node_pad), F32),
            pltpu.VMEM((1, node_pad), F32),
            pltpu.VMEM((8, terms), F32),
            pltpu.VMEM((peers, 8, terms), F32),
            pltpu.VMEM((3, bands, terms), F32),
            pltpu.VMEM((3, peers, bands, terms), F32),
            pltpu.VMEM((3, 2, bands, face_pad), F32),
            pltpu.VMEM((3, 2, bands, face_pad), F32),
            pltpu.VMEM((2, bands, node_pad // 2), BF16),
            pltpu.VMEM((n_band, bands, node_pad // 2), BF16),
            pltpu.VMEM((n_band, bands, bands), F32),
            pltpu.VMEM((n_band, bands, bands), F32),
            pltpu.VMEM((n_cell, bands, n_band * bands), F32),
            dma((2, peers)),
            dma((2, 3, peers)),
            dma((2, 3, 2)),
            dma((2, n_band - 1)),
            dma((2, n_band - 1)),
            dma((2, n_cell - 1)),
        ],
        compiler_params=pltpu.CompilerParams(
            collective_id=0, has_side_effects=True, vmem_limit_bytes=48 * 1024 * 1024
        ),
    )(
        waves,
        cell_matrix,
        node_map,
        share_list.reshape(share_list.shape[1:]),
        contacts,
        proj_values,
        coupling.T,
        proj_count.reshape(1, -1),
        mass.reshape(1, -1),
    )


def solution(mesh):
    return jax.shard_map(
        on_device,
        mesh=mesh,
        in_specs=(
            P("band", "cell"),
            P("cell", None, None),
            P("cell", None),
            P("cell", None, None),
            P(None, "cell"),
            P("cell", None, None),
            P(),
            P(),
            P("cell"),
        ),
        out_specs=(P("band", "cell"), P("band", None)),
        check_vma=False,
    )
```
